32 devices in a mesh: seq: 8 (over z, y), expert: 4 (over x, core).
Axes of the slice: x: 2, y: 2, z: 4, core: 2. Of those that a mesh axis runs over, the one named last changes fastest.
Arguments:
- residual: bfloat16 [4096, 2304], P(('seq', 'expert')), may hold values from -6 to 6
- query_rows: bfloat16 [4096, 4096], P('seq', 'expert'), may hold values from -6 to 6
- key_rows: bfloat16 [4096, 4096], P('seq', 'expert'), may hold values from -6 to 6
- value_rows: bfloat16 [4096, 4096], P('seq', 'expert'), may hold values from -6 to 6
- log_decay: float32 [4096, 4096], P('seq', 'expert'), may hold values from -0.7 to 0
- write_rate: float32 [4096, 32], P('seq', 'expert'), may hold values from 0 to 1
- output_weight: bfloat16 [4096, 2304], P('expert'), may hold values from -0.09375 to 0.09375
- routes: int32 [4096, 8], P(('seq', 'expert')), may hold values from 0 to 31, all different within a row; in each aligned block of 128 rows (0 to 127, 128 to 255, ...) at most 64 rows name the same one
- route_gates: float32 [4096, 8], P(('seq', 'expert')), may hold values from 0.1 to 0.6
- expert_up: bfloat16 [32, 2304, 1024], P(('seq', 'expert')), may hold values from -0.125 to 0.125
- expert_down: bfloat16 [32, 512, 2304], P(('seq', 'expert')), may hold values from -0.25 to 0.25
Outputs:
- layer_out: bfloat16 [4096, 2304], P(('seq', 'expert'))
The draws below stay inside these ranges and needn't reach their ends.
Inputs may be any that keep to these rules, and one draw needn't show every extreme that they name: `routes`: each row names 8 different experts. In each aligned block of 128 rows no expert is named by more than 64 rows, and in some block one expert is named by exactly 64.
All inputs are finite; a program needn't handle non-finite values.
Results may differ from the reference program's by a relative error of at most 0.007.
Values may be sent and summed in bfloat16 or wider, within the bound.
A program may use at most 128 MiB of HBM per device.

```python
import math
import jax
import jax.numpy as jnp
import numpy as np
from jax import lax

D = 2304
HEADS = 32
DK = 128
FFW = 512
TOP = 8
TOKENS = 4096
ROWS = 128
EXPERTS = 32
CAP = 64


def head_speed(key):
    chance = jax.random.uniform(jax.random.fold_in(key, 11), (HEADS,), jnp.float32)
    limit = 0.5
    return jnp.where(chance < limit, 1.0, 0.0).astype(jnp.float32)


def spread_log(key, shape, low, high):
    return jnp.exp(jax.random.uniform(key, shape, jnp.float32, math.log(low), math.log(high)))


def draw_key_rows(key, part):
    direction = jax.random.normal(jax.random.fold_in(key, 41), (1, HEADS, DK), jnp.float32)
    noise_part = jax.random.normal(jax.random.fold_in(key, 42), (TOKENS, HEADS, DK), jnp.float32)
    combined = jnp.clip(2.5 * direction + noise_part, -6.0, 6.0)
    return combined.reshape(TOKENS, HEADS * DK).astype(jnp.bfloat16)


def draw_log_decay(key, part):
    slow = head_speed(key)[:, None]
    fast_rate = spread_log(jax.random.fold_in(key, 21), (HEADS, DK), 1.0 / 60.0, 1.0 / 20.0)
    slow_rate = spread_log(jax.random.fold_in(key, 22), (HEADS, DK), 0.05 / TOKENS, 0.5 / TOKENS)
    write_strength = slow * slow_rate + (1.0 - slow) * fast_rate
    random_noise = spread_log(jax.random.fold_in(key, 23), (TOKENS, HEADS, DK), 0.5, 2.0)
    leading_slot_rank = jax.random.randint(jax.random.fold_in(key, 24), (HEADS,), 0, TOKENS)
    step_apart = jax.random.randint(jax.random.fold_in(key, 26), (HEADS,), 1, TOKENS)
    runner_slot_rank = (leading_slot_rank + step_apart) % TOKENS
    retained_entries = jax.random.uniform(jax.random.fold_in(key, 25), (2, HEADS), jnp.float32, 0.55, 0.8)
    slot_ranks = jnp.arange(TOKENS)[:, None]
    spike_amount = jnp.where(slot_ranks == leading_slot_rank[None, :], jnp.log(retained_entries[0])[None, :], 0.0)
    spike_amount = spike_amount + jnp.where(slot_ranks == runner_slot_rank[None, :], jnp.log(retained_entries[1])[None, :], 0.0)
    routed_output = -write_strength[None, :, :] * random_noise + spike_amount[:, :, None]
    return routed_output.reshape(TOKENS, HEADS * DK).astype(jnp.float32)


def draw_write_rate(key, part):
    slow = head_speed(key)[None, :]
    fast = jax.random.uniform(jax.random.fold_in(key, 31), (TOKENS, HEADS), jnp.float32, 0.2, 0.9)
    slow_part = 0.3 * DK / TOKENS * spread_log(jax.random.fold_in(key, 32), (TOKENS, HEADS), 0.5, 2.0)
    return (slow * slow_part + (1.0 - slow) * fast).astype(jnp.float32)


def level_of(rng, dims, cuts, least, top_value):
    level, own = 1.0, jax.random.fold_in(rng, 6)
    for dim, shards_of in cuts:
        draws = jnp.exp(jax.random.uniform(jax.random.fold_in(own, dim), (shards_of,), jnp.float32, least / len(cuts), top_value / len(cuts)))
        level = level * jnp.repeat(draws, dims[dim] // shards_of).reshape([-1 if axis == dim else 1 for axis in range(len(dims))])
    return level


def assign_block(rng, own, number, rows, amount, top, most, skew):
    order = jax.random.permutation(rng, amount)
    crowded, ordinary = portions_of(amount, rows * top, most, skew, True), portions_of(amount, rows * top, most, skew, False)
    places = jnp.arange(amount)

    def named(tallies, turn):
        used = int((tallies > 0).sum())
        fixed = max(1, used // 4)
        passed = fixed + (places - fixed + turn * (used - fixed)) % max(1, amount - fixed)
        return jnp.zeros((amount,), jnp.int32).at[order[jnp.where(places < fixed, places, passed)]].set(jnp.asarray(tallies, jnp.int32))

    tallies = jnp.where(number % 4 == 0, named(crowded, number // 4), named(ordinary, number - number // 4 - 1))
    mixed = jax.random.permutation(jax.random.fold_in(own, 3), amount)
    donor, taker = mixed[0:amount // 2 * 2:2], mixed[1:amount // 2 * 2:2]
    room = jnp.minimum(tallies[donor] - 1, most - tallies[taker]) // 2
    room = jnp.where((donor == order[0]) | (taker == order[0]) | (tallies[taker] == 0), 0, jnp.maximum(room, 0))
    passed = jax.random.randint(jax.random.fold_in(own, 4), (amount // 2,), 0, 1 << 20) % (room + 1)
    tallies = tallies.at[donor].add(-passed).at[taker].add(passed)
    items = jnp.searchsorted(jnp.cumsum(tallies), jnp.arange(rows * top), side="right").astype(jnp.int32)
    table = items.reshape(top, rows).T
    table = table[jax.random.permutation(jax.random.fold_in(own, 1), rows)]
    turn = jax.random.randint(jax.random.fold_in(own, 2), (rows, 1), 0, top)
    return jnp.take_along_axis(table, (jnp.arange(top)[None, :] + turn) % top, axis=1)


def portions_of(number_of, total, most, lean, full):
    weights = [(1 << 20) // math.isqrt(rank ** lean) + 1 for rank in range(1, number_of + 1)]
    largest = most if full else min(most, max(-(-total // number_of), total * weights[0] // sum(weights)))
    least = 1 if total - largest >= number_of - 1 else 0
    holding, surplus = [largest] + [least] * (number_of - 1), total - largest - least * (number_of - 1)
    while surplus > 0:
        movable = [i for i in range(1, number_of) if holding[i] < largest] or [i for i in range(1, number_of) if holding[i] < most]
        whole, budget = sum([weights[i] for i in movable]), surplus
        for i in movable:
            more = min(most - holding[i], max(1, budget * weights[i] // whole), surplus)
            holding[i] = holding[i] + more
            surplus = surplus - more
    return np.array(holding)


def scatter_about(rng, extent, deviation, most, split=(), held_as=jnp.bfloat16):
    result = deviation * jax.random.normal(rng, extent, jnp.float32)
    if split:
        result = result * level_of(rng, extent, split, -0.22, 0.18)
    return jnp.clip(result, -most, most).astype(held_as)


def setup_inputs(seed: int = 0) -> dict:
    splits = jax.random.split(jax.random.key(seed), 12)
    residual = scatter_about(splits[0], (TOKENS, D), 1.0, 6.0, ((0, 32),))
    query_rows = scatter_about(splits[1], (TOKENS, HEADS * DK), 1.0, 6.0, ((0, 8), (1, 4)))
    key_rows = draw_key_rows(jax.random.fold_in(splits[11], 71), 0)
    value_rows = scatter_about(splits[3], (TOKENS, HEADS * DK), 1.0, 6.0, ((0, 8), (1, 4)))
    log_decay = draw_log_decay(jax.random.fold_in(splits[11], 71), 0)
    write_rate = draw_write_rate(jax.random.fold_in(splits[11], 71), 0)
    output_weight = scatter_about(splits[6], (HEADS * DK, D), (HEADS * DK) ** -0.5, 0.09375, ((0, 4),))
    routes_keys = jax.random.split(jax.random.fold_in(splits[7], 1), TOKENS // ROWS)
    routes_turns = jax.random.permutation(jax.random.fold_in(splits[7], 3), TOKENS // ROWS)
    routes = jax.vmap(lambda own, number: assign_block(jax.random.fold_in(splits[7], 2), own, number, ROWS, EXPERTS, TOP, CAP, 2))(routes_keys, routes_turns).reshape((TOKENS, TOP))
    route_gates = jnp.clip(0.1 + 0.5 * jax.random.uniform(splits[8], (TOKENS, TOP), jnp.float32) ** level_of(splits[8], (TOKENS, TOP), ((0, 32),), -0.2, 0.2), 0.1, 0.6)
    expert_up = scatter_about(splits[9], (EXPERTS, D, 2 * FFW), D ** -0.5, 0.125, ((0, 32),))
    expert_down = scatter_about(splits[10], (EXPERTS, FFW, D), FFW ** -0.5, 0.25, ((0, 32),))
    return dict(residual=residual, query_rows=query_rows, key_rows=key_rows, value_rows=value_rows, log_decay=log_decay, write_rate=write_rate, output_weight=output_weight, routes=routes, route_gates=route_gates, expert_up=expert_up, expert_down=expert_down)


def unit_rows(block):
    return block * lax.rsqrt(lax.optimization_barrier(jnp.sum(block * block, axis=-1, keepdims=True)) + 1e-06)

def reference(residual, query_rows, key_rows, value_rows, log_decay, write_rate, output_weight, routes, route_gates, expert_up, expert_down):
    precise = lax.Precision.HIGHEST
    queries = unit_rows(query_rows.astype(jnp.float32).reshape(TOKENS, HEADS, DK))
    keyed = unit_rows(key_rows.astype(jnp.float32).reshape(TOKENS, HEADS, DK))
    values = value_rows.astype(jnp.float32).reshape(TOKENS, HEADS, DK)
    decays = jnp.exp(log_decay.reshape(TOKENS, HEADS, DK))

    def advance(state, inputs):
        query_now, key_now, value_now, decay_now, rate_now = inputs
        state = state * decay_now[:, :, None]
        recalled = jnp.einsum('hd,hde->he', key_now, state, precision=precise)
        state = state + rate_now[:, None, None] * key_now[:, :, None] * (value_now - recalled)[:, None, :]
        return (state, jnp.einsum('hd,hde->he', query_now, state, precision=precise))
    initial = jnp.zeros((HEADS, DK, DK), jnp.float32)
    final_state, head_out = lax.scan(advance, initial, (queries, keyed, values, decays, write_rate))
    head_norm = head_out * lax.rsqrt(lax.optimization_barrier(jnp.mean(head_out * head_out, axis=-1, keepdims=True)) + 1e-06)
    head_norm = head_norm.astype(jnp.bfloat16).reshape(TOKENS, HEADS * DK)
    attended = jnp.dot(head_norm, output_weight, preferred_element_type=jnp.float32)
    mixed = (residual.astype(jnp.float32) + attended).astype(jnp.bfloat16)
    mixed_wide = mixed.astype(jnp.float32)
    expert_in = (mixed_wide * lax.rsqrt(lax.optimization_barrier(jnp.mean(mixed_wide * mixed_wide, axis=-1, keepdims=True)) + 1e-06)).astype(jnp.bfloat16)
    pair_expert = routes.reshape(-1).astype(jnp.int32)
    pair_token = (jnp.arange(TOKENS * TOP) // TOP).astype(jnp.int32)
    source = (pair_token // ROWS).astype(jnp.int32)
    sort_key = (source * EXPERTS + pair_expert).astype(jnp.int32)
    order = jnp.argsort(sort_key, stable=True).astype(jnp.int32)
    sorted_key = sort_key[order]
    leading_slot_rank = jnp.searchsorted(sorted_key, sorted_key, side='left').astype(jnp.int32)
    sorted_rank = (jnp.arange(TOKENS * TOP).astype(jnp.int32) - leading_slot_rank).astype(jnp.int32)
    rank = jnp.zeros((TOKENS * TOP,), jnp.int32).at[order].set(sorted_rank)
    slot = (source * CAP + rank).astype(jnp.int32)
    token_table = jnp.full((EXPERTS, EXPERTS * CAP), TOKENS, jnp.int32).at[pair_expert, slot].set(pair_token)
    gate_table = jnp.zeros((EXPERTS, EXPERTS * CAP), jnp.float32).at[pair_expert, slot].set(route_gates.reshape(-1).astype(jnp.float32))
    padded = jnp.concatenate([expert_in, jnp.zeros((1, D), jnp.bfloat16)], axis=0)

    def run_expert(total, inputs):
        token_ids, gate_values, weight_up, weight_down = inputs
        rows_in = padded[token_ids]
        gate_up = jnp.dot(rows_in, weight_up, preferred_element_type=jnp.float32)
        hidden = (jax.nn.silu(gate_up[:, :FFW]) * gate_up[:, FFW:]).astype(jnp.bfloat16)
        routed_output = jnp.dot(hidden, weight_down, preferred_element_type=jnp.float32).astype(jnp.bfloat16)
        total = total.at[token_ids].add(gate_values[:, None] * routed_output.astype(jnp.float32))
        return (total, None)
    start_total = jnp.zeros((TOKENS + 1, D), jnp.float32)
    total, unused = lax.scan(run_expert, start_total, (token_table, gate_table, expert_up, expert_down))
    return (mixed_wide + total[:TOKENS]).astype(jnp.bfloat16)
```

```python
import jax
import jax.numpy as jnp
from jax import lax
from jax.sharding import PartitionSpec as P

BLOCK = 64


precise = lax.Precision.HIGH


def unit_rows(block):
    return block * lax.rsqrt(jnp.sum(block * block, axis=-1, keepdims=True) + 1e-06)


def head_blocks(array, heads):
    tokens = array.shape[0]
    width = array.shape[1] // heads
    shaped = array.reshape(tokens // BLOCK, BLOCK, heads, width)
    return jnp.transpose(shaped, (2, 0, 1, 3))


def unit_lower_inverse(lower_part):
    positions = jnp.arange(BLOCK)

    def off_diagonal(size):
        same = (positions[:, None] // (2 * size)) == (positions[None, :] // (2 * size))
        inner = (positions[:, None] // size) == (positions[None, :] // size)
        return jnp.where(same & ~inner, lower_part, 0.0)

    inverse = jnp.eye(BLOCK, dtype=jnp.float32) - off_diagonal(1)
    size = 2
    while size < BLOCK:
        part = jnp.einsum("hnst,hntu->hnsu", off_diagonal(size), inverse, precision=precise)
        inverse = inverse - jnp.einsum("hnst,hntu->hnsu", inverse, part, precision=precise)
        size *= 2
    return inverse


def block_terms(query_rows, key_rows, value_rows, log_decay, write_rate):
    heads = write_rate.shape[1]
    queries = unit_rows(head_blocks(query_rows.astype(jnp.float32), heads))
    keyed = unit_rows(head_blocks(key_rows.astype(jnp.float32), heads))
    values = head_blocks(value_rows.astype(jnp.float32), heads)
    rates = head_blocks(write_rate, heads)[..., 0]
    summed = jnp.cumsum(head_blocks(log_decay, heads), axis=2)
    middle = summed[:, :, BLOCK // 2 - 1 : BLOCK // 2, :]
    rising = jnp.exp(summed - middle)
    falling = jnp.exp(middle - summed)
    total_decay = summed[:, :, BLOCK - 1 :, :]
    key_down = keyed * falling
    scores = jnp.einsum("hnsd,hntd->hnst", keyed * rising, key_down, precision=precise)
    positions = jnp.arange(BLOCK)
    strict = positions[:, None] > positions[None, :]
    causal = positions[:, None] >= positions[None, :]
    lower_part = jnp.where(strict, scores * rates[..., None], 0.0)
    from_start = keyed * jnp.exp(summed)
    right_side = jnp.concatenate(
        [values * rates[..., None], from_start * rates[..., None]], axis=-1
    )
    inverse = unit_lower_inverse(lower_part)
    solved = jnp.einsum("hnst,hnte->hnse", inverse, right_side, precision=precise)
    value_width = values.shape[-1]
    fresh = solved[..., :value_width]
    carried = solved[..., value_width:]
    reach = jnp.where(
        causal, jnp.einsum("hnsd,hntd->hnst", queries * rising, key_down, precision=precise), 0.0
    )
    to_end = keyed * jnp.exp(total_decay - summed)
    key_width = keyed.shape[-1]
    transit = jnp.eye(key_width, dtype=jnp.float32) * jnp.exp(total_decay)[:, :, 0, :, None]
    transit = transit - jnp.einsum("hncd,hnce->hnde", to_end, carried, precision=precise)
    offset = jnp.einsum("hncd,hnce->hnde", to_end, fresh, precision=precise)
    exposure = queries * jnp.exp(summed) - jnp.einsum(
        "hnst,hntd->hnsd", reach, carried, precision=precise
    )
    direct = jnp.einsum("hnst,hnte->hnse", reach, fresh, precision=precise)
    return (transit, offset, exposure, direct)


def shard_chain(transit, offset, exposure, direct):
    heads, blocks, key_width = transit.shape[:3]
    value_width = offset.shape[-1]
    pair = jnp.concatenate(
        [
            jnp.broadcast_to(jnp.eye(key_width, dtype=jnp.float32), (heads, key_width, key_width)),
            jnp.zeros((heads, key_width, value_width), jnp.float32),
        ],
        axis=-1,
    )
    pairs = []
    for block in range(blocks):
        pairs.append(pair)
        pair = jnp.einsum("hij,hjk->hik", transit[:, block], pair, precision=precise)
        pair = pair.at[:, :, key_width:].add(offset[:, block])
    pairs = jnp.stack(pairs, axis=1)
    seen = jnp.einsum("hnsd,hnde->hnse", exposure, pairs, precision=precise)
    return (pair, seen[..., :key_width], seen[..., key_width:] + direct)


def incoming_states(pair):
    heads, key_width = pair.shape[:2]
    value_width = pair.shape[2] - key_width
    shards = lax.axis_size("seq")
    if heads == shards:
        mine = lax.all_to_all(pair, "seq", split_axis=0, concat_axis=0, tiled=True)
        state = jnp.zeros((key_width, value_width), jnp.float32)
        states = []
        for index in range(shards):
            states.append(state)
            if index < shards - 1:
                state = (
                    jnp.dot(mine[index, :, :key_width], state, precision=precise)
                    + mine[index, :, key_width:]
                )
        return lax.all_to_all(
            jnp.stack(states), "seq", split_axis=0, concat_axis=0, tiled=True
        )
    gathered = lax.all_gather(pair, "seq", axis=0, tiled=False)

    def absorb(index, current):
        return (
            jnp.einsum("hij,hjk->hik", gathered[index, :, :, :key_width], current, precision=precise)
            + gathered[index, :, :, key_width:]
        )

    return lax.fori_loop(
        0,
        lax.axis_index("seq"),
        absorb,
        jnp.zeros((heads, key_width, value_width), jnp.float32),
    )


def expert_rows(rows_in, expert_up, expert_down):
    hidden_width = expert_down.shape[0]
    gate_up = jnp.dot(rows_in, expert_up, preferred_element_type=jnp.float32)
    hidden = (jax.nn.silu(gate_up[:, :hidden_width]) * gate_up[:, hidden_width:]).astype(
        jnp.bfloat16
    )
    return jnp.dot(hidden, expert_down, preferred_element_type=jnp.float32).astype(jnp.bfloat16)


def routed_by_gather(expert_in, routes, route_gates, expert_up, expert_down):
    axes = ("seq", "expert")
    experts = lax.axis_size("seq") * lax.axis_size("expert")
    named = routes[:, :, None] == jnp.arange(experts, dtype=jnp.int32)[None, None, :]
    table = jnp.sum(jnp.where(named, route_gates[:, :, None], 0.0), axis=1)
    table = lax.all_gather(table, axes, axis=0, tiled=True)
    own = lax.axis_index("seq") * lax.axis_size("expert") + lax.axis_index("expert")
    gates = lax.dynamic_slice_in_dim(table, own, 1, axis=1)
    tokens = lax.all_gather(expert_in, axes, axis=0, tiled=True)
    results = expert_rows(tokens, expert_up[0], expert_down[0])
    share = (results.astype(jnp.float32) * gates).astype(jnp.bfloat16)
    return lax.psum_scatter(share, axes, scatter_dimension=0, tiled=True).astype(jnp.float32)


def routed_by_pairs(expert_in, routes, route_gates, expert_up, expert_down):
    seq_count = lax.axis_size("seq")
    lane_count = lax.axis_size("expert")
    experts = seq_count * lane_count
    chosen = routes.shape[1]
    rows = expert_in.shape[0]
    capacity = 2 * rows * chosen // experts
    width = expert_in.shape[1]
    flat_routes = routes.reshape(-1)
    member = (flat_routes[:, None] == jnp.arange(experts, dtype=jnp.int32)[None, :]).astype(
        jnp.int32
    )
    earlier = jnp.sum((jnp.cumsum(member, axis=0) - member) * member, axis=1)
    slots = flat_routes * capacity + earlier
    sources = jnp.arange(rows * chosen, dtype=jnp.int32) // chosen
    outgoing = (
        jnp.zeros((experts * capacity, width), jnp.bfloat16).at[slots].set(expert_in[sources])
    )
    outgoing = outgoing.reshape(seq_count, lane_count, capacity, width)
    arrived = lax.all_to_all(
        lax.all_to_all(outgoing, "seq", split_axis=0, concat_axis=0, tiled=True),
        "expert",
        split_axis=1,
        concat_axis=1,
        tiled=True,
    ).reshape(-1, width)
    results = expert_rows(arrived, expert_up[0], expert_down[0])
    results = results.reshape(seq_count, lane_count, capacity, width)
    returned = lax.all_to_all(
        lax.all_to_all(results, "seq", split_axis=0, concat_axis=0, tiled=True),
        "expert",
        split_axis=1,
        concat_axis=1,
        tiled=True,
    ).reshape(experts * capacity, width)
    picked = returned[slots].astype(jnp.float32) * route_gates.reshape(-1)[:, None]
    return jnp.sum(picked.reshape(rows, chosen, width), axis=1)

def per_device(
    residual,
    query_rows,
    key_rows,
    value_rows,
    log_decay,
    write_rate,
    output_weight,
    routes,
    route_gates,
    expert_up,
    expert_down,
):
    transit, offset, exposure, direct = block_terms(
        query_rows, key_rows, value_rows, log_decay, write_rate
    )
    pair, weights_in, local_outs = shard_chain(transit, offset, exposure, direct)
    heads = pair.shape[0]
    value_width = local_outs.shape[-1]
    incoming = incoming_states(pair)
    head_out = local_outs + jnp.einsum("hnsd,hde->hnse", weights_in, incoming, precision=precise)
    head_norm = head_out * lax.rsqrt(jnp.mean(head_out * head_out, axis=-1, keepdims=True) + 1e-06)
    head_norm = head_norm.astype(jnp.bfloat16)
    tokens = query_rows.shape[0]
    head_norm = jnp.transpose(head_norm, (1, 2, 0, 3)).reshape(tokens, heads * value_width)
    attended = lax.psum_scatter(
        jnp.dot(head_norm, output_weight, preferred_element_type=jnp.float32).astype(jnp.bfloat16),
        "expert",
        scatter_dimension=0,
        tiled=True,
    ).astype(jnp.float32)
    mixed = (residual.astype(jnp.float32) + attended).astype(jnp.bfloat16)
    mixed_wide = mixed.astype(jnp.float32)
    expert_in = (
        mixed_wide * lax.rsqrt(jnp.mean(mixed_wide * mixed_wide, axis=-1, keepdims=True) + 1e-06)
    ).astype(jnp.bfloat16)
    experts = lax.axis_size("seq") * lax.axis_size("expert")
    chosen = routes.shape[1]
    routed = routed_by_gather if experts <= 4 * chosen else routed_by_pairs
    combined = routed(expert_in, routes, route_gates, expert_up, expert_down)
    return (mixed_wide + combined).astype(jnp.bfloat16)


def solution(mesh):
    return jax.shard_map(
        per_device,
        mesh=mesh,
        in_specs=(
            P(("seq", "expert"), None),
            P("seq", "expert"),
            P("seq", "expert"),
            P("seq", "expert"),
            P("seq", "expert"),
            P("seq", "expert"),
            P("expert", None),
            P(("seq", "expert"), None),
            P(("seq", "expert"), None),
            P(("seq", "expert"), None, None),
            P(("seq", "expert"), None, None),
        ),
        out_specs=P(("seq", "expert"), None),
        check_vma=False,
    )
```

```python
import jax
import jax.numpy as jnp
from jax import lax
from jax.sharding import PartitionSpec as P

BLOCK = 64
PARTS = 2


precise = lax.Precision.HIGH


def unit_rows(block):
    return block * lax.rsqrt(jnp.sum(block * block, axis=-1, keepdims=True) + 1e-06)


def head_blocks(array, heads):
    tokens = array.shape[0]
    width = array.shape[1] // heads
    shaped = array.reshape(tokens // BLOCK, BLOCK, heads, width)
    return jnp.transpose(shaped, (2, 0, 1, 3))


def unit_lower_inverse(lower_part):
    positions = jnp.arange(BLOCK)

    def off_diagonal(size):
        same = (positions[:, None] // (2 * size)) == (positions[None, :] // (2 * size))
        inner = (positions[:, None] // size) == (positions[None, :] // size)
        return jnp.where(same & ~inner, lower_part, 0.0)

    inverse = jnp.eye(BLOCK, dtype=jnp.float32) - off_diagonal(1)
    size = 2
    while size < BLOCK:
        part = jnp.einsum("hnst,hntu->hnsu", off_diagonal(size), inverse, precision=precise)
        inverse = inverse - jnp.einsum("hnst,hntu->hnsu", inverse, part, precision=precise)
        size *= 2
    return inverse


def block_terms(query_rows, key_rows, value_rows, log_decay, write_rate):
    heads = write_rate.shape[1]
    queries = unit_rows(head_blocks(query_rows.astype(jnp.float32), heads))
    keyed = unit_rows(head_blocks(key_rows.astype(jnp.float32), heads))
    values = head_blocks(value_rows.astype(jnp.float32), heads)
    rates = head_blocks(write_rate, heads)[..., 0]
    summed = jnp.cumsum(head_blocks(log_decay, heads), axis=2)
    middle = summed[:, :, BLOCK // 2 - 1 : BLOCK // 2, :]
    rising = jnp.exp(summed - middle)
    falling = jnp.exp(middle - summed)
    total_decay = summed[:, :, BLOCK - 1 :, :]
    key_down = keyed * falling
    scores = jnp.einsum("hnsd,hntd->hnst", keyed * rising, key_down, precision=precise)
    positions = jnp.arange(BLOCK)
    strict = positions[:, None] > positions[None, :]
    causal = positions[:, None] >= positions[None, :]
    lower_part = jnp.where(strict, scores * rates[..., None], 0.0)
    from_start = keyed * jnp.exp(summed)
    right_side = jnp.concatenate(
        [values * rates[..., None], from_start * rates[..., None]], axis=-1
    )
    inverse = unit_lower_inverse(lower_part)
    solved = jnp.einsum("hnst,hnte->hnse", inverse, right_side, precision=precise)
    value_width = values.shape[-1]
    fresh = solved[..., :value_width]
    carried = solved[..., value_width:]
    reach = jnp.where(
        causal, jnp.einsum("hnsd,hntd->hnst", queries * rising, key_down, precision=precise), 0.0
    )
    to_end = keyed * jnp.exp(total_decay - summed)
    key_width = keyed.shape[-1]
    transit = jnp.eye(key_width, dtype=jnp.float32) * jnp.exp(total_decay)[:, :, 0, :, None]
    transit = transit - jnp.einsum("hncd,hnce->hnde", to_end, carried, precision=precise)
    offset = jnp.einsum("hncd,hnce->hnde", to_end, fresh, precision=precise)
    exposure = queries * jnp.exp(summed) - jnp.einsum(
        "hnst,hntd->hnsd", reach, carried, precision=precise
    )
    direct = jnp.einsum("hnst,hnte->hnse", reach, fresh, precision=precise)
    return (transit, offset, exposure, direct)


def shard_chain(transit, offset, exposure, direct):
    heads, blocks, key_width = transit.shape[:3]
    value_width = offset.shape[-1]
    pair = jnp.concatenate(
        [
            jnp.broadcast_to(jnp.eye(key_width, dtype=jnp.float32), (heads, key_width, key_width)),
            jnp.zeros((heads, key_width, value_width), jnp.float32),
        ],
        axis=-1,
    )
    pairs = []
    for block in range(blocks):
        pairs.append(pair)
        pair = jnp.einsum("hij,hjk->hik", transit[:, block], pair, precision=precise)
        pair = pair.at[:, :, key_width:].add(offset[:, block])
    pairs = jnp.stack(pairs, axis=1)
    seen = jnp.einsum("hnsd,hnde->hnse", exposure, pairs, precision=precise)
    return (pair, seen[..., :key_width], seen[..., key_width:] + direct)


def incoming_states(pair):
    heads, key_width = pair.shape[:2]
    value_width = pair.shape[2] - key_width
    shards = lax.axis_size("seq")
    if heads == shards:
        mine = lax.all_to_all(pair, "seq", split_axis=0, concat_axis=0, tiled=True)
        state = jnp.zeros((key_width, value_width), jnp.float32)
        states = []
        for index in range(shards):
            states.append(state)
            if index < shards - 1:
                state = (
                    jnp.dot(mine[index, :, :key_width], state, precision=precise)
                    + mine[index, :, key_width:]
                )
        return lax.all_to_all(
            jnp.stack(states), "seq", split_axis=0, concat_axis=0, tiled=True
        )
    gathered = lax.all_gather(pair, "seq", axis=0, tiled=False)

    def absorb(index, current):
        return (
            jnp.einsum("hij,hjk->hik", gathered[index, :, :, :key_width], current, precision=precise)
            + gathered[index, :, :, key_width:]
        )

    return lax.fori_loop(
        0,
        lax.axis_index("seq"),
        absorb,
        jnp.zeros((heads, key_width, value_width), jnp.float32),
    )


def expert_rows(rows_in, expert_up, expert_down):
    hidden_width = expert_down.shape[0]
    gate_up = jnp.dot(rows_in, expert_up, preferred_element_type=jnp.float32)
    hidden = (jax.nn.silu(gate_up[:, :hidden_width]) * gate_up[:, hidden_width:]).astype(
        jnp.bfloat16
    )
    return jnp.dot(hidden, expert_down, preferred_element_type=jnp.float32).astype(jnp.bfloat16)


def lane_weights(weights):
    lanes = lax.axis_size("expert")
    held = {0: weights}
    step = lanes // 2
    while step >= 1:
        order = [(lane, lane ^ step) for lane in range(lanes)]
        for m in list(held):
            held[m ^ step] = tuple(lax.ppermute(part, "expert", order) for part in held[m])
        step //= 2
    return held


def lane_gates(routes, route_gates):
    shards, lanes = lax.axis_size("seq"), lax.axis_size("expert")
    numbers = jnp.arange(shards * lanes, dtype=jnp.int32)
    named = numbers[:, None, None] == routes.T[None, :, :]
    table = jnp.sum(jnp.where(named, route_gates.T[None, :, :], 0.0), axis=1)
    table = table.reshape(shards, lanes, routes.shape[0])
    return lax.all_to_all(table, "seq", split_axis=0, concat_axis=0, tiled=True)


def routed_by_gather(expert_in, gates, weights):
    rows, width = expert_in.shape
    shards = lax.axis_size("seq")
    lane = lax.axis_index("expert")
    part = rows // PARTS
    results = []
    for index in range(PARTS):
        own = expert_in[index * part : (index + 1) * part]
        tokens = lax.all_gather(own, "seq", axis=0, tiled=True)
        total = jnp.zeros((shards * part, width), jnp.float32)
        for m, (up, down) in weights.items():
            gate = lax.dynamic_index_in_dim(gates, lane ^ m, axis=1, keepdims=False)
            gate = gate[:, index * part : (index + 1) * part].reshape(-1, 1)
            total += gate * expert_rows(tokens, up[0], down[0]).astype(jnp.float32)
        results.append(
            lax.psum_scatter(total.astype(jnp.bfloat16), "seq", scatter_dimension=0, tiled=True)
        )
    return jnp.concatenate(results, axis=0).astype(jnp.float32)


def routed_by_pairs(expert_in, routes, route_gates, expert_up, expert_down):
    seq_count = lax.axis_size("seq")
    lane_count = lax.axis_size("expert")
    experts = seq_count * lane_count
    chosen = routes.shape[1]
    rows = expert_in.shape[0]
    capacity = 2 * rows * chosen // experts
    width = expert_in.shape[1]
    flat_routes = routes.reshape(-1)
    member = (flat_routes[:, None] == jnp.arange(experts, dtype=jnp.int32)[None, :]).astype(
        jnp.int32
    )
    earlier = jnp.sum((jnp.cumsum(member, axis=0) - member) * member, axis=1)
    slots = flat_routes * capacity + earlier
    sources = jnp.arange(rows * chosen, dtype=jnp.int32) // chosen
    outgoing = (
        jnp.zeros((experts * capacity, width), jnp.bfloat16).at[slots].set(expert_in[sources])
    )
    outgoing = outgoing.reshape(seq_count, lane_count, capacity, width)
    arrived = lax.all_to_all(
        lax.all_to_all(outgoing, "seq", split_axis=0, concat_axis=0, tiled=True),
        "expert",
        split_axis=1,
        concat_axis=1,
        tiled=True,
    ).reshape(-1, width)
    results = expert_rows(arrived, expert_up[0], expert_down[0])
    results = results.reshape(seq_count, lane_count, capacity, width)
    returned = lax.all_to_all(
        lax.all_to_all(results, "seq", split_axis=0, concat_axis=0, tiled=True),
        "expert",
        split_axis=1,
        concat_axis=1,
        tiled=True,
    ).reshape(experts * capacity, width)
    picked = returned[slots].astype(jnp.float32) * route_gates.reshape(-1)[:, None]
    return jnp.sum(picked.reshape(rows, chosen, width), axis=1)

def per_device(
    residual,
    query_rows,
    key_rows,
    value_rows,
    log_decay,
    write_rate,
    output_weight,
    routes,
    route_gates,
    expert_up,
    expert_down,
):
    experts = lax.axis_size("seq") * lax.axis_size("expert")
    by_gather = experts <= 4 * routes.shape[1]
    if by_gather:
        gates = lane_gates(routes, route_gates)
        weights = lane_weights((expert_up, expert_down))
    transit, offset, exposure, direct = block_terms(
        query_rows, key_rows, value_rows, log_decay, write_rate
    )
    pair, weights_in, local_outs = shard_chain(transit, offset, exposure, direct)
    heads = pair.shape[0]
    value_width = local_outs.shape[-1]
    incoming = incoming_states(pair)
    head_out = local_outs + jnp.einsum("hnsd,hde->hnse", weights_in, incoming, precision=precise)
    head_norm = head_out * lax.rsqrt(jnp.mean(head_out * head_out, axis=-1, keepdims=True) + 1e-06)
    head_norm = head_norm.astype(jnp.bfloat16)
    tokens = query_rows.shape[0]
    head_norm = jnp.transpose(head_norm, (1, 2, 0, 3)).reshape(tokens, heads * value_width)
    attended = lax.psum_scatter(
        jnp.dot(head_norm, output_weight, preferred_element_type=jnp.float32).astype(jnp.bfloat16),
        "expert",
        scatter_dimension=0,
        tiled=True,
    ).astype(jnp.float32)
    mixed = (residual.astype(jnp.float32) + attended).astype(jnp.bfloat16)
    mixed_wide = mixed.astype(jnp.float32)
    expert_in = (
        mixed_wide * lax.rsqrt(jnp.mean(mixed_wide * mixed_wide, axis=-1, keepdims=True) + 1e-06)
    ).astype(jnp.bfloat16)
    if by_gather:
        combined = routed_by_gather(expert_in, gates, weights)
    else:
        combined = routed_by_pairs(expert_in, routes, route_gates, expert_up, expert_down)
    return (mixed_wide + combined).astype(jnp.bfloat16)


def solution(mesh):
    return jax.shard_map(
        per_device,
        mesh=mesh,
        in_specs=(
            P(("seq", "expert"), None),
            P("seq", "expert"),
            P("seq", "expert"),
            P("seq", "expert"),
            P("seq", "expert"),
            P("seq", "expert"),
            P("expert", None),
            P(("seq", "expert"), None),
            P(("seq", "expert"), None),
            P(("seq", "expert"), None, None),
            P(("seq", "expert"), None, None),
        ),
        out_specs=P(("seq", "expert"), None),
        check_vma=False,
    )
```

```python
import jax
import jax.numpy as jnp
from jax import lax
from jax.sharding import PartitionSpec as P

BLOCK = 64
PARTS = 2


precise = lax.Precision.HIGH


def unit_rows(block):
    return block * lax.rsqrt(jnp.sum(block * block, axis=-1, keepdims=True) + 1e-06)


def head_blocks(array, heads):
    tokens = array.shape[0]
    width = array.shape[1] // heads
    shaped = array.reshape(tokens // BLOCK, BLOCK, heads, width)
    return jnp.transpose(shaped, (2, 0, 1, 3))


def unit_lower_inverse(lower_part):
    positions = jnp.arange(BLOCK)

    def off_diagonal(size):
        same = (positions[:, None] // (2 * size)) == (positions[None, :] // (2 * size))
        inner = (positions[:, None] // size) == (positions[None, :] // size)
        return jnp.where(same & ~inner, lower_part, 0.0)

    inverse = jnp.eye(BLOCK, dtype=jnp.float32) - off_diagonal(1)
    size = 2
    while size < BLOCK:
        part = jnp.einsum("hnst,hntu->hnsu", off_diagonal(size), inverse, precision=precise)
        inverse = inverse - jnp.einsum("hnst,hntu->hnsu", inverse, part, precision=precise)
        size *= 2
    return inverse


def block_terms(query_rows, key_rows, value_rows, log_decay, write_rate):
    heads = write_rate.shape[1]
    queries = unit_rows(head_blocks(query_rows.astype(jnp.float32), heads))
    keyed = unit_rows(head_blocks(key_rows.astype(jnp.float32), heads))
    values = head_blocks(value_rows.astype(jnp.float32), heads)
    rates = head_blocks(write_rate, heads)[..., 0]
    summed = jnp.cumsum(head_blocks(log_decay, heads), axis=2)
    middle = summed[:, :, BLOCK // 2 - 1 : BLOCK // 2, :]
    rising = jnp.exp(summed - middle)
    falling = jnp.exp(middle - summed)
    total_decay = summed[:, :, BLOCK - 1 :, :]
    key_down = keyed * falling
    scores = jnp.einsum("hnsd,hntd->hnst", keyed * rising, key_down, precision=precise)
    positions = jnp.arange(BLOCK)
    strict = positions[:, None] > positions[None, :]
    causal = positions[:, None] >= positions[None, :]
    lower_part = jnp.where(strict, scores * rates[..., None], 0.0)
    from_start = keyed * jnp.exp(summed)
    right_side = jnp.concatenate(
        [values * rates[..., None], from_start * rates[..., None]], axis=-1
    )
    inverse = unit_lower_inverse(lower_part)
    solved = jnp.einsum("hnst,hnte->hnse", inverse, right_side, precision=precise)
    value_width = values.shape[-1]
    fresh = solved[..., :value_width]
    carried = solved[..., value_width:]
    reach = jnp.where(
        causal, jnp.einsum("hnsd,hntd->hnst", queries * rising, key_down, precision=precise), 0.0
    )
    to_end = keyed * jnp.exp(total_decay - summed)
    key_width = keyed.shape[-1]
    transit = jnp.eye(key_width, dtype=jnp.float32) * jnp.exp(total_decay)[:, :, 0, :, None]
    transit = transit - jnp.einsum("hncd,hnce->hnde", to_end, carried, precision=precise)
    offset = jnp.einsum("hncd,hnce->hnde", to_end, fresh, precision=precise)
    exposure = queries * jnp.exp(summed) - jnp.einsum(
        "hnst,hntd->hnsd", reach, carried, precision=precise
    )
    direct = jnp.einsum("hnst,hnte->hnse", reach, fresh, precision=precise)
    return (transit, offset, exposure, direct)


def shard_chain(transit, offset, exposure, direct):
    heads, blocks, key_width = transit.shape[:3]
    value_width = offset.shape[-1]
    pair = jnp.concatenate(
        [
            jnp.broadcast_to(jnp.eye(key_width, dtype=jnp.float32), (heads, key_width, key_width)),
            jnp.zeros((heads, key_width, value_width), jnp.float32),
        ],
        axis=-1,
    )
    pairs = []
    for block in range(blocks):
        pairs.append(pair)
        pair = jnp.einsum("hij,hjk->hik", transit[:, block], pair, precision=precise)
        pair = pair.at[:, :, key_width:].add(offset[:, block])
    pairs = jnp.stack(pairs, axis=1)
    seen = jnp.einsum("hnsd,hnde->hnse", exposure, pairs, precision=precise)
    return (pair, seen[..., :key_width], seen[..., key_width:] + direct)


def incoming_states(pair):
    heads, key_width = pair.shape[:2]
    value_width = pair.shape[2] - key_width
    shards = lax.axis_size("seq")
    if heads == shards:
        mine = lax.all_to_all(pair, "seq", split_axis=0, concat_axis=0, tiled=True)
        state = jnp.zeros((key_width, value_width), jnp.float32)
        states = []
        for index in range(shards):
            states.append(state)
            if index < shards - 1:
                state = (
                    jnp.dot(mine[index, :, :key_width], state, precision=precise)
                    + mine[index, :, key_width:]
                )
        return lax.all_to_all(
            jnp.stack(states), "seq", split_axis=0, concat_axis=0, tiled=True
        )
    gathered = lax.all_gather(pair, "seq", axis=0, tiled=False)

    def absorb(index, current):
        return (
            jnp.einsum("hij,hjk->hik", gathered[index, :, :, :key_width], current, precision=precise)
            + gathered[index, :, :, key_width:]
        )

    return lax.fori_loop(
        0,
        lax.axis_index("seq"),
        absorb,
        jnp.zeros((heads, key_width, value_width), jnp.float32),
    )


def expert_rows(rows_in, expert_up, expert_down):
    hidden_width = expert_down.shape[0]
    gate_up = jnp.dot(rows_in, expert_up, preferred_element_type=jnp.float32)
    hidden = (jax.nn.silu(gate_up[:, :hidden_width]) * gate_up[:, hidden_width:]).astype(
        jnp.bfloat16
    )
    return jnp.dot(hidden, expert_down, preferred_element_type=jnp.float32).astype(jnp.bfloat16)


def tie(value, moved):
    return lax.optimization_barrier((value, moved))


def far_lane(part):
    lanes = lax.axis_size("expert")
    return lax.ppermute(part, "expert", [(lane, lane ^ (lanes // 2)) for lane in range(lanes)])


def lane_weights(held):
    lanes = lax.axis_size("expert")
    step = lanes // 4
    while step >= 1:
        order = [(lane, lane ^ step) for lane in range(lanes)]
        for m in list(held):
            held[m ^ step] = tuple(lax.ppermute(part, "expert", order) for part in held[m])
        step //= 2
    return held


def halve(blocks, axis, step):
    size = lax.axis_size(axis)
    bit = (lax.axis_index(axis) // step) % 2
    pairs = blocks.reshape((blocks.shape[0] // 2, 2) + blocks.shape[1:])
    given = lax.dynamic_index_in_dim(pairs, 1 - bit, axis=1, keepdims=False)
    kept = lax.dynamic_index_in_dim(pairs, bit, axis=1, keepdims=False)
    order = [(place, place ^ step) for place in range(size)]
    return kept + lax.ppermute(given.astype(jnp.bfloat16), axis, order).astype(jnp.float32)


def sum_lanes(blocks):
    step = 1
    while step < lax.axis_size("expert"):
        blocks = halve(blocks, "expert", step)
        step *= 2
    return blocks[0]


def sum_line(blocks):
    size = lax.axis_size("seq")
    count = blocks.shape[0]
    inner = size // count
    place = lax.axis_index("seq") // inner
    result = lax.dynamic_index_in_dim(blocks, place, axis=0, keepdims=False)
    for way in (1, -1):
        moving = None
        for far in range(count - 1, 0, -1):
            block = lax.dynamic_index_in_dim(
                blocks, jnp.clip(place + way * far, 0, count - 1), axis=0, keepdims=False
            )
            moving = block if moving is None else block + moving
            order = [
                (index, index + way * inner)
                for index in range(size)
                if 0 <= index // inner + way * far < count
            ]
            moving = lax.ppermute(moving.astype(jnp.bfloat16), "seq", order).astype(jnp.float32)
        result = result + moving
    return result


def sum_shards(total):
    size = lax.axis_size("seq")
    part = total.shape[0] // size
    half = total.shape[1] // 2
    first = halve(total[:, :half].reshape(size, part, half), "seq", 1)
    first = sum_line(first)
    second = sum_line(total[:, half:].reshape(size // 2, 2 * part, half))
    second = halve(second.reshape(2, part, half), "seq", 1)[0]
    return jnp.concatenate([first, second], axis=1)


def lane_gates(routes, route_gates):
    shards, lanes = lax.axis_size("seq"), lax.axis_size("expert")
    numbers = jnp.arange(shards * lanes, dtype=jnp.int32)
    named = numbers[:, None, None] == routes.T[None, :, :]
    table = jnp.sum(jnp.where(named, route_gates.T[None, :, :], 0.0), axis=1)
    table = table.reshape(shards, lanes, routes.shape[0])
    return lax.all_to_all(table, "seq", split_axis=0, concat_axis=0, tiled=True)


def routed_by_gather(expert_in, gates, weights):
    rows, width = expert_in.shape
    shards = lax.axis_size("seq")
    lane = lax.axis_index("expert")
    part = rows // PARTS
    results = []
    for index in range(PARTS):
        own = expert_in[index * part : (index + 1) * part]
        tokens = lax.all_gather(own, "seq", axis=0, tiled=True)
        total = jnp.zeros((shards * part, width), jnp.float32)
        for m, (up, down) in weights.items():
            gate = lax.dynamic_index_in_dim(gates, lane ^ m, axis=1, keepdims=False)
            gate = gate[:, index * part : (index + 1) * part].reshape(-1, 1)
            total += gate * expert_rows(tokens, up[0], down[0]).astype(jnp.float32)
        results.append(sum_shards(total))
    return jnp.concatenate(results, axis=0)


def routed_by_pairs(expert_in, routes, route_gates, expert_up, expert_down):
    seq_count = lax.axis_size("seq")
    lane_count = lax.axis_size("expert")
    experts = seq_count * lane_count
    chosen = routes.shape[1]
    rows = expert_in.shape[0]
    capacity = 2 * rows * chosen // experts
    width = expert_in.shape[1]
    flat_routes = routes.reshape(-1)
    member = (flat_routes[:, None] == jnp.arange(experts, dtype=jnp.int32)[None, :]).astype(
        jnp.int32
    )
    earlier = jnp.sum((jnp.cumsum(member, axis=0) - member) * member, axis=1)
    slots = flat_routes * capacity + earlier
    sources = jnp.arange(rows * chosen, dtype=jnp.int32) // chosen
    outgoing = (
        jnp.zeros((experts * capacity, width), jnp.bfloat16).at[slots].set(expert_in[sources])
    )
    outgoing = outgoing.reshape(seq_count, lane_count, capacity, width)
    arrived = lax.all_to_all(
        lax.all_to_all(outgoing, "seq", split_axis=0, concat_axis=0, tiled=True),
        "expert",
        split_axis=1,
        concat_axis=1,
        tiled=True,
    ).reshape(-1, width)
    results = expert_rows(arrived, expert_up[0], expert_down[0])
    results = results.reshape(seq_count, lane_count, capacity, width)
    returned = lax.all_to_all(
        lax.all_to_all(results, "seq", split_axis=0, concat_axis=0, tiled=True),
        "expert",
        split_axis=1,
        concat_axis=1,
        tiled=True,
    ).reshape(experts * capacity, width)
    picked = returned[slots].astype(jnp.float32) * route_gates.reshape(-1)[:, None]
    return jnp.sum(picked.reshape(rows, chosen, width), axis=1)

def per_device(
    residual,
    query_rows,
    key_rows,
    value_rows,
    log_decay,
    write_rate,
    output_weight,
    routes,
    route_gates,
    expert_up,
    expert_down,
):
    experts = lax.axis_size("seq") * lax.axis_size("expert")
    by_gather = experts <= 4 * routes.shape[1]
    if by_gather:
        gates = lane_gates(routes, route_gates)
        middle = expert_up.shape[1] // 2
        far_up = [far_lane(expert_up[:, :middle]), far_lane(expert_up[:, middle:])]
        far_down = far_lane(expert_down)
    transit, offset, exposure, direct = block_terms(
        query_rows, key_rows, value_rows, log_decay, write_rate
    )
    pair, weights_in, local_outs = shard_chain(transit, offset, exposure, direct)
    heads = pair.shape[0]
    value_width = local_outs.shape[-1]
    if by_gather:
        pair, far_up[0] = tie(pair, far_up[0])
    incoming = incoming_states(pair)
    if by_gather:
        incoming, far_up[1] = tie(incoming, far_up[1])
    head_out = local_outs + jnp.einsum("hnsd,hde->hnse", weights_in, incoming, precision=precise)
    head_norm = head_out * lax.rsqrt(jnp.mean(head_out * head_out, axis=-1, keepdims=True) + 1e-06)
    head_norm = head_norm.astype(jnp.bfloat16)
    tokens = query_rows.shape[0]
    head_norm = jnp.transpose(head_norm, (1, 2, 0, 3)).reshape(tokens, heads * value_width)
    projected = jnp.dot(head_norm, output_weight, preferred_element_type=jnp.float32)
    attended = sum_lanes(projected.reshape((-1,) + residual.shape))
    if by_gather:
        attended, far_down = tie(attended, far_down)
        weights = lane_weights(
            {
                0: (expert_up, expert_down),
                lax.axis_size("expert") // 2: (jnp.concatenate(far_up, axis=1), far_down),
            }
        )
    mixed = (residual.astype(jnp.float32) + attended).astype(jnp.bfloat16)
    mixed_wide = mixed.astype(jnp.float32)
    expert_in = (
        mixed_wide * lax.rsqrt(jnp.mean(mixed_wide * mixed_wide, axis=-1, keepdims=True) + 1e-06)
    ).astype(jnp.bfloat16)
    if by_gather:
        combined = routed_by_gather(expert_in, gates, weights)
    else:
        combined = routed_by_pairs(expert_in, routes, route_gates, expert_up, expert_down)
    return (mixed_wide + combined).astype(jnp.bfloat16)


def solution(mesh):
    return jax.shard_map(
        per_device,
        mesh=mesh,
        in_specs=(
            P(("seq", "expert"), None),
            P("seq", "expert"),
            P("seq", "expert"),
            P("seq", "expert"),
            P("seq", "expert"),
            P("seq", "expert"),
            P("expert", None),
            P(("seq", "expert"), None),
            P(("seq", "expert"), None),
            P(("seq", "expert"), None, None),
            P(("seq", "expert"), None, None),
        ),
        out_specs=P(("seq", "expert"), None),
        check_vma=False,
    )
```

```python
import jax
import jax.numpy as jnp
from jax import lax
from jax.sharding import PartitionSpec as P

BLOCK = 64
PARTS = 2


precise = lax.Precision.HIGH


def unit_rows(block):
    return block * lax.rsqrt(jnp.sum(block * block, axis=-1, keepdims=True) + 1e-06)


def head_blocks(array, heads):
    tokens = array.shape[0]
    width = array.shape[1] // heads
    shaped = array.reshape(tokens // BLOCK, BLOCK, heads, width)
    return jnp.transpose(shaped, (2, 0, 1, 3))


def unit_lower_inverse(lower_part):
    positions = jnp.arange(BLOCK)

    def off_diagonal(size):
        same = (positions[:, None] // (2 * size)) == (positions[None, :] // (2 * size))
        inner = (positions[:, None] // size) == (positions[None, :] // size)
        return jnp.where(same & ~inner, lower_part, 0.0)

    inverse = jnp.eye(BLOCK, dtype=jnp.float32) - off_diagonal(1)
    size = 2
    while size < BLOCK:
        part = jnp.einsum("hnst,hntu->hnsu", off_diagonal(size), inverse, precision=precise)
        inverse = inverse - jnp.einsum("hnst,hntu->hnsu", inverse, part, precision=precise)
        size *= 2
    return inverse


def block_terms(query_rows, key_rows, value_rows, log_decay, write_rate):
    heads = write_rate.shape[1]
    queries = unit_rows(head_blocks(query_rows.astype(jnp.float32), heads))
    keyed = unit_rows(head_blocks(key_rows.astype(jnp.float32), heads))
    values = head_blocks(value_rows.astype(jnp.float32), heads)
    rates = head_blocks(write_rate, heads)[..., 0]
    summed = jnp.cumsum(head_blocks(log_decay, heads), axis=2)
    middle = summed[:, :, BLOCK // 2 - 1 : BLOCK // 2, :]
    rising = jnp.exp(summed - middle)
    falling = jnp.exp(middle - summed)
    total_decay = summed[:, :, BLOCK - 1 :, :]
    key_down = keyed * falling
    scores = jnp.einsum("hnsd,hntd->hnst", keyed * rising, key_down, precision=precise)
    positions = jnp.arange(BLOCK)
    strict = positions[:, None] > positions[None, :]
    causal = positions[:, None] >= positions[None, :]
    lower_part = jnp.where(strict, scores * rates[..., None], 0.0)
    from_start = keyed * jnp.exp(summed)
    right_side = jnp.concatenate(
        [values * rates[..., None], from_start * rates[..., None]], axis=-1
    )
    inverse = unit_lower_inverse(lower_part)
    solved = jnp.einsum("hnst,hnte->hnse", inverse, right_side, precision=precise)
    value_width = values.shape[-1]
    fresh = solved[..., :value_width]
    carried = solved[..., value_width:]
    reach = jnp.where(
        causal, jnp.einsum("hnsd,hntd->hnst", queries * rising, key_down, precision=precise), 0.0
    )
    to_end = keyed * jnp.exp(total_decay - summed)
    key_width = keyed.shape[-1]
    transit = jnp.eye(key_width, dtype=jnp.float32) * jnp.exp(total_decay)[:, :, 0, :, None]
    transit = transit - jnp.einsum("hncd,hnce->hnde", to_end, carried, precision=precise)
    offset = jnp.einsum("hncd,hnce->hnde", to_end, fresh, precision=precise)
    exposure = queries * jnp.exp(summed) - jnp.einsum(
        "hnst,hntd->hnsd", reach, carried, precision=precise
    )
    direct = jnp.einsum("hnst,hnte->hnse", reach, fresh, precision=precise)
    return (transit, offset, exposure, direct)


def shard_chain(transit, offset, exposure, direct):
    heads, blocks, key_width = transit.shape[:3]
    value_width = offset.shape[-1]
    pair = jnp.concatenate(
        [
            jnp.broadcast_to(jnp.eye(key_width, dtype=jnp.float32), (heads, key_width, key_width)),
            jnp.zeros((heads, key_width, value_width), jnp.float32),
        ],
        axis=-1,
    )
    pairs = []
    for block in range(blocks):
        pairs.append(pair)
        pair = jnp.einsum("hij,hjk->hik", transit[:, block], pair, precision=precise)
        pair = pair.at[:, :, key_width:].add(offset[:, block])
    pairs = jnp.stack(pairs, axis=1)
    seen = jnp.einsum("hnsd,hnde->hnse", exposure, pairs, precision=precise)
    return (pair, seen[..., :key_width], seen[..., key_width:] + direct)


def incoming_states(pair):
    heads, key_width = pair.shape[:2]
    value_width = pair.shape[2] - key_width
    shards = lax.axis_size("seq")
    if heads == shards:
        mine = lax.all_to_all(pair, "seq", split_axis=0, concat_axis=0, tiled=True)
        state = jnp.zeros((key_width, value_width), jnp.float32)
        states = []
        for index in range(shards):
            states.append(state)
            if index < shards - 1:
                state = (
                    jnp.dot(mine[index, :, :key_width], state, precision=precise)
                    + mine[index, :, key_width:]
                )
        return lax.all_to_all(
            jnp.stack(states), "seq", split_axis=0, concat_axis=0, tiled=True
        )
    gathered = lax.all_gather(pair, "seq", axis=0, tiled=False)

    def absorb(index, current):
        return (
            jnp.einsum("hij,hjk->hik", gathered[index, :, :, :key_width], current, precision=precise)
            + gathered[index, :, :, key_width:]
        )

    return lax.fori_loop(
        0,
        lax.axis_index("seq"),
        absorb,
        jnp.zeros((heads, key_width, value_width), jnp.float32),
    )


def expert_rows(rows_in, expert_up, expert_down):
    hidden_width = expert_down.shape[0]
    gate_up = jnp.dot(rows_in, expert_up, preferred_element_type=jnp.float32)
    hidden = (jax.nn.silu(gate_up[:, :hidden_width]) * gate_up[:, hidden_width:]).astype(
        jnp.bfloat16
    )
    return jnp.dot(hidden, expert_down, preferred_element_type=jnp.float32).astype(jnp.bfloat16)


def tie(value, moved):
    return lax.optimization_barrier((value, moved))


def far_lane(part):
    lanes = lax.axis_size("expert")
    return lax.ppermute(part, "expert", [(lane, lane ^ (lanes // 2)) for lane in range(lanes)])


def lane_weights(held):
    lanes = lax.axis_size("expert")
    step = lanes // 4
    while step >= 1:
        order = [(lane, lane ^ step) for lane in range(lanes)]
        for m in list(held):
            held[m ^ step] = tuple(lax.ppermute(part, "expert", order) for part in held[m])
        step //= 2
    return held


def halve(blocks, axis, step):
    size = lax.axis_size(axis)
    bit = (lax.axis_index(axis) // step) % 2
    pairs = blocks.reshape((blocks.shape[0] // 2, 2) + blocks.shape[1:])
    given = lax.dynamic_index_in_dim(pairs, 1 - bit, axis=1, keepdims=False)
    kept = lax.dynamic_index_in_dim(pairs, bit, axis=1, keepdims=False)
    order = [(place, place ^ step) for place in range(size)]
    return kept + lax.ppermute(given.astype(jnp.bfloat16), axis, order).astype(jnp.float32)


def sum_lanes(blocks):
    step = 1
    while step < lax.axis_size("expert"):
        blocks = halve(blocks, "expert", step)
        step *= 2
    return blocks[0]


def sum_line(blocks):
    size = lax.axis_size("seq")
    count = blocks.shape[0]
    inner = size // count
    place = lax.axis_index("seq") // inner
    result = lax.dynamic_index_in_dim(blocks, place, axis=0, keepdims=False)
    for way in (1, -1):
        moving = None
        for far in range(count - 1, 0, -1):
            block = lax.dynamic_index_in_dim(
                blocks, jnp.clip(place + way * far, 0, count - 1), axis=0, keepdims=False
            )
            moving = block if moving is None else block + moving
            order = [
                (index, index + way * inner)
                for index in range(size)
                if 0 <= index // inner + way * far < count
            ]
            moving = lax.ppermute(moving.astype(jnp.bfloat16), "seq", order).astype(jnp.float32)
        result = result + moving
    return result


def sum_shards(total):
    size = lax.axis_size("seq")
    part = total.shape[0] // size
    half = total.shape[1] // 2
    first = halve(total[:, :half].reshape(size, part, half), "seq", 1)
    first = sum_line(first)
    second = sum_line(total[:, half:].reshape(size // 2, 2 * part, half))
    second = halve(second.reshape(2, part, half), "seq", 1)[0]
    return jnp.concatenate([first, second], axis=1)


def lane_gates(routes, route_gates):
    shards, lanes = lax.axis_size("seq"), lax.axis_size("expert")
    numbers = jnp.arange(shards * lanes, dtype=jnp.int32)
    named = numbers[:, None, None] == routes.T[None, :, :]
    table = jnp.sum(jnp.where(named, route_gates.T[None, :, :], 0.0), axis=1)
    table = table.reshape(shards, lanes, routes.shape[0])
    return lax.all_to_all(table, "seq", split_axis=0, concat_axis=0, tiled=True)


def routed_by_gather(expert_in, gates, weights):
    rows, width = expert_in.shape
    shards = lax.axis_size("seq")
    lane = lax.axis_index("expert")
    part = rows // PARTS
    results = []
    for index in range(PARTS):
        own = expert_in[index * part : (index + 1) * part]
        tokens = lax.all_gather(own, "seq", axis=0, tiled=True)
        total = jnp.zeros((shards * part, width), jnp.float32)
        for m, (up, down) in weights.items():
            gate = lax.dynamic_index_in_dim(gates, lane ^ m, axis=1, keepdims=False)
            gate = gate[:, index * part : (index + 1) * part].reshape(-1, 1)
            total += gate * expert_rows(tokens, up[0], down[0]).astype(jnp.float32)
        results.append(sum_shards(total))
    return jnp.concatenate(results, axis=0)


def routed_by_pairs(expert_in, routes, route_gates, expert_up, expert_down):
    seq_count = lax.axis_size("seq")
    lane_count = lax.axis_size("expert")
    experts = seq_count * lane_count
    chosen = routes.shape[1]
    rows = expert_in.shape[0]
    capacity = 2 * rows * chosen // experts
    width = expert_in.shape[1]
    flat_routes = routes.reshape(-1)
    member = (flat_routes[:, None] == jnp.arange(experts, dtype=jnp.int32)[None, :]).astype(
        jnp.int32
    )
    earlier = jnp.sum((jnp.cumsum(member, axis=0) - member) * member, axis=1)
    slots = flat_routes * capacity + earlier
    sources = jnp.arange(rows * chosen, dtype=jnp.int32) // chosen
    outgoing = (
        jnp.zeros((experts * capacity, width), jnp.bfloat16).at[slots].set(expert_in[sources])
    )
    outgoing = outgoing.reshape(seq_count, lane_count, capacity, width)
    arrived = lax.all_to_all(
        lax.all_to_all(outgoing, "seq", split_axis=0, concat_axis=0, tiled=True),
        "expert",
        split_axis=1,
        concat_axis=1,
        tiled=True,
    ).reshape(-1, width)
    results = expert_rows(arrived, expert_up[0], expert_down[0])
    results = results.reshape(seq_count, lane_count, capacity, width)
    returned = lax.all_to_all(
        lax.all_to_all(results, "seq", split_axis=0, concat_axis=0, tiled=True),
        "expert",
        split_axis=1,
        concat_axis=1,
        tiled=True,
    ).reshape(experts * capacity, width)
    picked = returned[slots].astype(jnp.float32) * route_gates.reshape(-1)[:, None]
    return jnp.sum(picked.reshape(rows, chosen, width), axis=1)

def per_device(
    residual,
    query_rows,
    key_rows,
    value_rows,
    log_decay,
    write_rate,
    output_weight,
    routes,
    route_gates,
    expert_up,
    expert_down,
):
    experts = lax.axis_size("seq") * lax.axis_size("expert")
    by_gather = experts <= 4 * routes.shape[1]
    if by_gather:
        gates = lane_gates(routes, route_gates)
        middle = expert_up.shape[1] // 2
        far_up = [far_lane(expert_up[:, :middle]), far_lane(expert_up[:, middle:])]
        far_down = far_lane(expert_down)
    transit, offset, exposure, direct = block_terms(
        query_rows, key_rows, value_rows, log_decay, write_rate
    )
    pair, weights_in, local_outs = shard_chain(transit, offset, exposure, direct)
    heads = pair.shape[0]
    value_width = local_outs.shape[-1]
    if by_gather:
        pair, far_up[0] = tie(pair, far_up[0])
    incoming = incoming_states(pair)
    if by_gather:
        incoming, far_up[1] = tie(incoming, far_up[1])
    head_out = local_outs + jnp.einsum("hnsd,hde->hnse", weights_in, incoming, precision=precise)
    head_norm = head_out * lax.rsqrt(jnp.mean(head_out * head_out, axis=-1, keepdims=True) + 1e-06)
    head_norm = head_norm.astype(jnp.bfloat16)
    tokens = query_rows.shape[0]
    head_norm = jnp.transpose(head_norm, (1, 2, 0, 3)).reshape(tokens, heads * value_width)
    projected = jnp.dot(head_norm, output_weight, preferred_element_type=jnp.float32)
    if by_gather:
        projected, far_down = tie(projected, far_down)
    attended = sum_lanes(projected.reshape((-1,) + residual.shape))
    if by_gather:
        weights = lane_weights(
            {
                0: (expert_up, expert_down),
                lax.axis_size("expert") // 2: (jnp.concatenate(far_up, axis=1), far_down),
            }
        )
    mixed = (residual.astype(jnp.float32) + attended).astype(jnp.bfloat16)
    mixed_wide = mixed.astype(jnp.float32)
    expert_in = (
        mixed_wide * lax.rsqrt(jnp.mean(mixed_wide * mixed_wide, axis=-1, keepdims=True) + 1e-06)
    ).astype(jnp.bfloat16)
    if by_gather:
        combined = routed_by_gather(expert_in, gates, weights)
    else:
        combined = routed_by_pairs(expert_in, routes, route_gates, expert_up, expert_down)
    return (mixed_wide + combined).astype(jnp.bfloat16)


def solution(mesh):
    return jax.shard_map(
        per_device,
        mesh=mesh,
        in_specs=(
            P(("seq", "expert"), None),
            P("seq", "expert"),
            P("seq", "expert"),
            P("seq", "expert"),
            P("seq", "expert"),
            P("seq", "expert"),
            P("expert", None),
            P(("seq", "expert"), None),
            P(("seq", "expert"), None),
            P(("seq", "expert"), None, None),
            P(("seq", "expert"), None, None),
        ),
        out_specs=P(("seq", "expert"), None),
        check_vma=False,
    )
```
